32 devices in a mesh: seq: 4 (over y, core), buf: 8 (over z, x).
Axes of the slice: x: 2, y: 2, z: 4, core: 2. Of those that a mesh axis runs over, the one named last changes fastest.
Arguments:
- row_inputs: bfloat16 [64, 128, 1024], P(('seq', 'buf')), may hold values from -6 to 6
- row_shared: bfloat16 [64, 128, 128], P(('seq', 'buf')), may hold values from -4 to 4
- row_steps: bfloat16 [64, 128, 16], P(('seq', 'buf')), may hold values from -3 to 3
- row_count: int32 [32], P(('seq', 'buf')), may hold values from 0 to 2, as said below
- row_slot: int32 [64], P(('seq', 'buf')), may hold values from 0 to 47, as said below
- doc_start: int32 [6144], P('seq'), may hold values from 0 to 1, as said below
- decay_log: float32 [16], P('buf'), may hold values from -9.2 to 2.78
- step_bias: float32 [16], P('buf'), may hold values from -6.92 to -3.89
- skip_gain: float32 [16], P('buf'), may hold values from 0.5 to 1.5
Outputs:
- mixer_out: bfloat16 [6144, 1024], P('seq', 'buf')
The draws below stay inside these ranges and needn't reach their ends.
Inputs may be any that keep to these rules, and one draw needn't show every extreme that they name: `row_count`: over the 8 hosts of one sequence shard the counts sum to 12; in every shard some host holds 2 live buffers. `row_slot`: A live buffer's stream row lies in its host's own sequence shard (rows 12 * s to 12 * s + 11 for shard s), and the live buffers of a shard fill each of its rows exactly once; entries of buffers that are not live are arbitrary rows of the same shard. `doc_start`: there are max(1, 1) ones, one in each of as many consecutive sequence shards.
All inputs are finite; a program needn't handle non-finite values.
Results may differ from the reference program's by a relative error of at most 0.0065.
Values may be sent and summed in bfloat16 or wider, within the bound.
A program may use at most 64 MiB of HBM per device.

```python
import math
import jax
import jax.numpy as jnp
from jax import lax

P_SIZE = 64
NS = 64
SPAN = 256
ROW = 128
CAP = 2
SLOTS = 12
TOK_SHARD = 1536
TOKENS = 6144
HEADS = 16
INNER = 1024
HOSTS = 32
ROW_BUFFERS = 64


def seat_plan(key):
    shards = TOKENS // (SLOTS * ROW)
    hosts_per = HOSTS // shards
    seats = hosts_per * CAP

    def one_shard(shard):
        shard_key = jax.random.fold_in(key, shard)
        order = jax.random.permutation(jax.random.fold_in(shard_key, 1), seats)
        rank = jnp.zeros((seats,), jnp.int32).at[order].set(jnp.arange(seats, dtype=jnp.int32))
        center = jax.random.randint(jax.random.fold_in(shard_key, 2), (), 0, hosts_per)
        seat_host = jnp.arange(seats, dtype=jnp.int32) // CAP
        score = rank + jnp.where(seat_host == center, -seats, 0).astype(jnp.int32)
        picked_order = jnp.argsort(score, stable=True)
        picked = jnp.zeros((seats,), jnp.int32).at[picked_order[:SLOTS]].set(1)
        counts = jnp.sum(picked.reshape(hosts_per, CAP), axis=1).astype(jnp.int32)
        live_flag = (jnp.arange(CAP, dtype=jnp.int32)[None, :] < counts[:, None]).reshape(-1).astype(jnp.int32)
        position = jnp.cumsum(live_flag) - 1
        stream_order = jax.random.permutation(jax.random.fold_in(shard_key, 3), SLOTS).astype(jnp.int32)
        garbage = jax.random.randint(jax.random.fold_in(shard_key, 4), (seats,), 0, SLOTS)
        local_slot = jnp.where(live_flag == 1, stream_order[jnp.clip(position, 0, SLOTS - 1)], garbage)
        return (counts, (local_slot + shard * SLOTS).astype(jnp.int32))
    counts, slots = jax.vmap(one_shard)(jnp.arange(shards, dtype=jnp.int32))
    return (counts.reshape(-1), slots.reshape(-1))


def draw_row_count(key, part):
    counts, slots = seat_plan(jax.random.fold_in(key, 77))
    return counts


def draw_row_slot(key, part):
    counts, slots = seat_plan(jax.random.fold_in(key, 77))
    return slots


def draw_doc_start(key, part):
    key = jax.random.fold_in(key, 5)
    shards = TOKENS // TOK_SHARD
    marked = max(1, shards // 4)
    opening = jax.random.randint(jax.random.fold_in(key, 1), (), 0, shards - marked + 1)
    offsets = jax.random.randint(jax.random.fold_in(key, 2), (marked,), 0, TOK_SHARD)
    where_ones = ((opening + jnp.arange(marked, dtype=jnp.int32)) * TOK_SHARD + offsets).astype(jnp.int32)
    return jnp.zeros((TOKENS,), jnp.int32).at[where_ones].set(1)


def head_rates(key):
    base_key = jax.random.fold_in(key, 11)
    chooser = jax.random.uniform(jax.random.fold_in(base_key, 1), (HEADS,), jnp.float32)
    slow_share = 0.6
    is_slow = chooser < slow_share
    fast_rate = jax.random.uniform(jax.random.fold_in(base_key, 3), (HEADS,), jnp.float32, math.log(4.0), math.log(16.0))
    slow_step = jax.random.uniform(jax.random.fold_in(base_key, 4), (HEADS,), jnp.float32, math.log(0.001), math.log(0.002))
    fast_step = jax.random.uniform(jax.random.fold_in(base_key, 5), (HEADS,), jnp.float32, math.log(0.003), math.log(0.01))
    ratio_log = jax.random.uniform(jax.random.fold_in(base_key, 6), (HEADS,), jnp.float32, 0.0, math.log(2.0))
    chain_total = jax.random.uniform(jax.random.fold_in(base_key, 7), (HEADS,), jnp.float32, 0.3, 1.8)
    step_base = jnp.exp(jnp.where(is_slow, slow_step, fast_step) + ratio_log)
    slow_rate = jnp.log(chain_total / (step_base * (1.133 * TOKENS)))
    rate_log = jnp.where(is_slow, slow_rate, fast_rate)
    return (rate_log, step_base)


def draw_decay_log(key, part):
    rate_log, step_base = head_rates(key)
    return rate_log.astype(jnp.float32)


def draw_step_bias(key, part):
    rate_log, step_base = head_rates(key)
    return jnp.log(jnp.expm1(step_base)).astype(jnp.float32)


def levels(rng, dims, cuts, least, top_value):
    factor_of, own = 1.0, jax.random.fold_in(rng, 6)
    for dim, blocks in cuts:
        heights = jnp.exp(jax.random.uniform(jax.random.fold_in(own, dim), (blocks,), jnp.float32, least / len(cuts), top_value / len(cuts)))
        factor_of = factor_of * jnp.repeat(heights, dims[dim] // blocks).reshape([-1 if axis == dim else 1 for axis in range(len(dims))])
    return factor_of


def bell_draw(stream_key, shape, width, most, cuts=(), kind=jnp.bfloat16):
    values = jax.random.normal(stream_key, shape, jnp.float32) * width
    if len(cuts) > 0:
        values = levels(stream_key, shape, cuts, -0.22, 0.18) * values
    return jnp.clip(values, min=-most, max=most).astype(kind)


def setup_inputs(seed: int = 0) -> dict:
    key_of = jax.random.split(jax.random.key(seed), 10)
    return {
        "row_inputs": bell_draw(key_of[0], (ROW_BUFFERS, ROW, INNER), 1.0, 6.0, ((0, 32),)),
        "row_shared": bell_draw(key_of[1], (ROW_BUFFERS, ROW, 2 * NS), 1.0, 4.0, ((0, 32),)),
        "row_steps": bell_draw(key_of[2], (ROW_BUFFERS, ROW, HEADS), 0.5, 3.0, ((0, 32),)),
        "row_count": draw_row_count(jax.random.fold_in(key_of[9], 71), 0),
        "row_slot": draw_row_slot(jax.random.fold_in(key_of[9], 71), 0),
        "doc_start": draw_doc_start(jax.random.fold_in(key_of[9], 71), 0),
        "decay_log": draw_decay_log(jax.random.fold_in(key_of[9], 71), 0),
        "step_bias": draw_step_bias(jax.random.fold_in(key_of[9], 71), 0),
        "skip_gain": jnp.clip(1.0 + 0.1 * jax.random.normal(key_of[8], (HEADS,), jnp.float32), 0.5, 1.5),
    }


def span_parts(inputs, b_part, c_part, raw_steps, starts, decay_log, step_bias):
    length = inputs.shape[0]
    step_size = jax.nn.softplus(raw_steps.astype(jnp.float32) + step_bias)
    log_decay = -step_size * jnp.exp(decay_log)
    decay_sum = jnp.cumsum(log_decay, axis=0)
    reset_count = jnp.cumsum(starts, axis=0)
    scores = jnp.dot(c_part, b_part.T, preferred_element_type=jnp.float32)
    position = jnp.arange(length, dtype=jnp.int32)
    together = (reset_count[:, None] == reset_count[None, :]) & (position[:, None] >= position[None, :])
    gap_sum = decay_sum.T[:, :, None] - decay_sum.T[:, None, :]
    factor = jnp.where(together[None], jnp.exp(jnp.where(together[None], gap_sum, 0.0)), 0.0)
    weight = lax.optimization_barrier((scores[None] * factor * step_size.T[:, None, :]).astype(jnp.bfloat16))
    within_span = jnp.einsum("hts,shp->thp", weight.astype(jnp.float32), inputs.astype(jnp.float32))
    keep_tail = reset_count == reset_count[-1]
    tail_factor = jnp.where(keep_tail[:, None], jnp.exp(decay_sum[-1][None, :] - decay_sum), 0.0) * step_size
    weighted = lax.optimization_barrier((inputs.astype(jnp.float32) * tail_factor[:, :, None]).astype(jnp.bfloat16))
    span_state = jnp.einsum("shp,sn->hpn", weighted.astype(jnp.float32), b_part.astype(jnp.float32))
    pass_factor = jnp.where(reset_count[-1] == 0, jnp.exp(decay_sum[-1]), 0.0)
    entry_scale = jnp.where((reset_count == 0)[:, None], jnp.exp(decay_sum), 0.0)
    return within_span, span_state, pass_factor, entry_scale


def reference(row_inputs, row_shared, row_steps, row_count, row_slot, doc_start, decay_log, step_bias, skip_gain):
    stream_rows = TOKENS // ROW
    buffer_index = jnp.arange(row_slot.shape[0], dtype=jnp.int32)
    is_live = (buffer_index % CAP) < jnp.repeat(row_count, CAP)
    target = jnp.where(is_live, row_slot, stream_rows).astype(jnp.int32)
    source = jnp.zeros((stream_rows,), jnp.int32).at[target].set(buffer_index, mode="drop")
    spans = TOKENS // SPAN
    inputs = row_inputs[source].reshape(spans, SPAN, HEADS, P_SIZE)
    shared = row_shared[source].reshape(spans, SPAN, 2 * NS)
    raw_steps = row_steps[source].reshape(spans, SPAN, HEADS)
    starts = doc_start.reshape(spans, SPAN)

    def advance(incoming, pieces):
        span_inputs, span_shared, span_raw, span_starts = pieces
        b_part = span_shared[:, :NS]
        c_part = span_shared[:, NS:]
        within_span, span_state, pass_factor, entry_scale = span_parts(
            span_inputs, b_part, c_part, span_raw, span_starts, decay_log, step_bias)
        carried = lax.optimization_barrier(incoming.astype(jnp.bfloat16))
        from_state = jnp.einsum("tn,hpn->thp", c_part.astype(jnp.float32), carried.astype(jnp.float32))
        mixed = within_span + from_state * entry_scale[:, :, None] + skip_gain[None, :, None] * span_inputs.astype(jnp.float32)
        outgoing = pass_factor[:, None, None] * incoming + span_state
        return outgoing, mixed.astype(jnp.bfloat16).reshape(SPAN, HEADS * P_SIZE)

    start_state = jnp.zeros((HEADS, P_SIZE, NS), jnp.float32)
    final_state, mixed = lax.scan(advance, start_state, (inputs, shared, raw_steps, starts))
    return mixed.reshape(TOKENS, HEADS * P_SIZE)
```

```python
import functools

import jax
import jax.numpy as jnp
from jax import lax
from jax.experimental import pallas as pl
from jax.experimental.pallas import tpu as pltpu
from jax.sharding import PartitionSpec as P

MESH = pl.DeviceIdType.MESH
EXACT = lax.Precision.HIGHEST


def softplus(value):
    small = jnp.exp(-jnp.abs(value))
    ratio = small / (small + 2.0)
    square = ratio * ratio
    series = jnp.full_like(ratio, 1.0 / 17.0)
    for odd in (15.0, 13.0, 11.0, 9.0, 7.0, 5.0, 3.0, 1.0):
        series = series * square + 1.0 / odd
    return jnp.maximum(value, 0.0) + 2.0 * ratio * series


def kernel(
    n, ns, heads_dev, stream_rows,
    inputs_ref, shared_ref, steps_ref, count_ref, slot_ref, doc_ref, log_ref, bias_ref, gain_ref,
    out_ref,
    xbuf, sbuf, step_out, step_in, meta_out, meta_in, meta_smem, source,
    docs, cums, counts_in, steps_q, enters, tails, passes,
    ybuf, ebuf, span_state, row_pass, incoming, prior_pass, leave_out, leave_in,
    x_send, x_recv, s_send, s_recv, f_send, st_send, st_recv, m_send, m_recv, l_send, l_recv, own_sem,
):
    me = lax.axis_index("buf")
    sq = lax.axis_index("seq")
    bit = lax.rem(me, 2)
    partner = me + 1 - 2 * bit
    buffers, row_len = steps_ref.shape[0], steps_ref.shape[1]
    width = xbuf.shape[3]
    head_size = width // heads_dev
    state = sbuf.shape[3] // 2
    half = n // 2

    barrier = pltpu.get_barrier_semaphore()

    def greet_buf(j, carry):
        pl.semaphore_signal(barrier, inc=1, device_id={"buf": lax.rem(me + j, n)}, device_id_type=MESH)
        return carry

    def greet_seq(j, carry):
        pl.semaphore_signal(barrier, inc=1, device_id={"seq": lax.rem(sq + j, ns)}, device_id_type=MESH)
        return carry

    lax.fori_loop(1, n, greet_buf, 0)
    lax.fori_loop(1, ns, greet_seq, 0)

    own_x = pltpu.make_async_copy(
        inputs_ref.at[:, :, pl.ds(pl.multiple_of(me * width, width), width)], xbuf.at[0], own_sem.at[0])
    own_s = pltpu.make_async_copy(shared_ref, sbuf.at[0], own_sem.at[1])
    own_x.start()
    own_s.start()

    step_out[...] = jnp.zeros_like(step_out)
    for b in range(buffers):
        turned = steps_ref[b].astype(jnp.float32).T
        for g in range(n):
            step_out[g, b * heads_dev:(b + 1) * heads_dev, :] = turned[g * heads_dev:(g + 1) * heads_dev, :]
    count = count_ref[0]
    row_id = lax.broadcasted_iota(jnp.int32, meta_out.shape, 0)
    meta = jnp.full(meta_out.shape, stream_rows, jnp.int32)
    for b in range(buffers):
        slot = jnp.clip(slot_ref[b] - sq * stream_rows, 0, stream_rows - 1)
        meta = jnp.where(row_id == b, jnp.where(b < count, slot, stream_rows), meta)
    meta_out[...] = meta
    meta_in[0] = meta
    step_in[0] = step_out[me]

    pl.semaphore_wait(barrier, n - 1 + ns - 1)

    def x_copy(j):
        peer = lax.rem(me + j, n)
        return pltpu.make_async_remote_copy(
            src_ref=inputs_ref.at[:, :, pl.ds(pl.multiple_of(peer * width, width), width)],
            dst_ref=xbuf.at[j], send_sem=x_send.at[j], recv_sem=x_recv.at[j],
            device_id={"buf": peer}, device_id_type=MESH)

    def step_copy(j):
        peer = lax.rem(me + j, n)
        return pltpu.make_async_remote_copy(
            src_ref=step_out.at[peer], dst_ref=step_in.at[j], send_sem=st_send.at[j], recv_sem=st_recv.at[j],
            device_id={"buf": peer}, device_id_type=MESH)

    def meta_copy(j):
        peer = lax.rem(me + j, n)
        return pltpu.make_async_remote_copy(
            src_ref=meta_out, dst_ref=meta_in.at[j], send_sem=m_send.at[j], recv_sem=m_recv.at[j],
            device_id={"buf": peer}, device_id_type=MESH)

    def shared_copy(i):
        peer = lax.rem(me + 2 * i, n)
        return pltpu.make_async_remote_copy(
            src_ref=shared_ref, dst_ref=sbuf.at[2 * i], send_sem=s_send.at[i], recv_sem=s_recv.at[2 * i],
            device_id={"buf": peer}, device_id_type=MESH)

    def forward_copy(i, src):
        slot = lax.rem(2 * i + 1 - 2 * bit + n, n)
        return pltpu.make_async_remote_copy(
            src_ref=src, dst_ref=sbuf.at[slot], send_sem=f_send.at[i], recv_sem=s_recv.at[slot],
            device_id={"buf": partner}, device_id_type=MESH)

    def shared_arrival(j):
        return pltpu.make_async_remote_copy(
            src_ref=shared_ref, dst_ref=sbuf.at[j], send_sem=f_send.at[0], recv_sem=s_recv.at[j],
            device_id={"buf": partner}, device_id_type=MESH)

    def leave_copy(i):
        return pltpu.make_async_remote_copy(
            src_ref=leave_out, dst_ref=leave_in.at[i], send_sem=l_send.at[i], recv_sem=l_recv.at[i],
            device_id={"seq": lax.rem(sq + i, ns)}, device_id_type=MESH)

    def start_small(j, carry):
        meta_copy(j).start()
        step_copy(j).start()
        return carry

    def start_shared(i, carry):
        shared_copy(i).start()
        return carry

    def start_x(j, carry):
        x_copy(j).start()
        return carry

    lax.fori_loop(1, n, start_small, 0)
    lax.fori_loop(1, half, start_shared, 0)
    forward_copy(0, shared_ref).start()
    lax.fori_loop(1, n, start_x, 0)

    def wait_small(j, carry):
        meta_copy(j).wait_recv()
        step_copy(j).wait_recv()
        return carry

    lax.fori_loop(1, n, wait_small, 0)
    to_scalar = pltpu.make_async_copy(meta_in, meta_smem, own_sem.at[2])
    to_scalar.start()

    shape = (n * 8, row_len)
    tri_up = (lax.broadcasted_iota(jnp.int32, (row_len, row_len), 0)
              <= lax.broadcasted_iota(jnp.int32, (row_len, row_len), 1)).astype(jnp.float32)
    head_row = lax.rem(lax.broadcasted_iota(jnp.int32, shape, 0), heads_dev)
    bias = jnp.full(shape, bias_ref[0], jnp.float32)
    decay = jnp.full(shape, log_ref[0], jnp.float32)
    for h in range(1, heads_dev):
        bias = jnp.where(head_row == h, bias_ref[h], bias)
        decay = jnp.where(head_row == h, log_ref[h], decay)
    step = softplus(step_in[...].reshape(shape) + bias)
    cum = jnp.dot(-step * jnp.exp(decay), tri_up, precision=EXACT, preferred_element_type=jnp.float32)

    to_scalar.wait()
    docs[...] = jnp.zeros_like(docs)

    def put_docs(j, carry):
        for b in range(buffers):
            slot = jnp.minimum(meta_smem[j, b, 0], stream_rows - 1)
            line = doc_ref[pl.ds(slot, 1), :].astype(jnp.float32)
            docs[j, b * heads_dev:(b + 1) * heads_dev, :] = jnp.broadcast_to(line, (heads_dev, row_len))
        return carry

    lax.fori_loop(0, n, put_docs, 0)

    def put_source(k, carry):
        found = jnp.int32(0)
        for j in range(n):
            for b in range(buffers):
                found = found + jnp.where(meta_smem[j, b, 0] == k, j * buffers + b, 0)
        source[k] = found
        return carry

    lax.fori_loop(0, stream_rows, put_source, 0)

    resets = jnp.dot(docs[...].reshape(shape), tri_up, precision=EXACT, preferred_element_type=jnp.float32)
    last_cum = cum[:, row_len - 1:row_len]
    last_resets = resets[:, row_len - 1:row_len]
    cube = (n, 8, row_len)
    cums[...] = cum.reshape(cube)
    counts_in[...] = resets.reshape(cube)
    steps_q[...] = step.reshape(cube)
    enters[...] = jnp.where(resets == 0.0, jnp.exp(cum), 0.0).reshape(cube)
    tails[...] = (jnp.where(resets == last_resets, jnp.exp(last_cum - cum), 0.0) * step).reshape(cube)
    passes[...] = jnp.broadcast_to(
        jnp.where(last_resets == 0.0, jnp.exp(last_cum), 0.0), shape).reshape(cube)

    own_s.wait()

    def pass_on(i, carry):
        shared_arrival(2 * i).wait_recv()
        forward_copy(i, sbuf.at[2 * i]).start()
        return carry

    lax.fori_loop(1, half, pass_on, 0)
    own_x.wait()

    lower = (lax.broadcasted_iota(jnp.int32, (row_len, row_len), 0)
             >= lax.broadcasted_iota(jnp.int32, (row_len, row_len), 1))
    lane_head = lax.broadcasted_iota(jnp.int32, (1, width), 1) // head_size
    gain = jnp.full((1, width), gain_ref[0], jnp.float32)
    for h in range(1, heads_dev):
        gain = jnp.where(lane_head == h, gain_ref[h], gain)

    def by_head(parts):
        full = jnp.broadcast_to(parts[0], (parts[0].shape[0], width))
        for h in range(1, heads_dev):
            full = jnp.where(lane_head == h, parts[h], full)
        return full

    def do_peer(j):
        cum_j = cums[j]
        resets_j = counts_in[j]
        step_j = steps_q[j]
        pass_j = passes[j]
        turned = jnp.concatenate([cum_j, resets_j, enters[j], tails[j]], axis=0).T
        for b in range(buffers):
            r = j * buffers + b
            x = xbuf[j, b]
            wide = x.astype(jnp.float32)
            b_part = sbuf[j, b, :, :state]
            c_part = sbuf[j, b, :, state:]
            scores = lax.dot_general(c_part, b_part, (((1,), (1,)), ((), ())),
                                     preferred_element_type=jnp.float32)
            q = b * heads_dev
            together = lower & (turned[:, 8 + q:9 + q] == resets_j[q:q + 1, :])
            weights = []
            masked = []
            for h in range(heads_dev):
                gap = turned[:, q + h:q + h + 1] - cum_j[q + h:q + h + 1, :]
                factor = jnp.exp(jnp.where(together, gap, -1e30))
                weights.append((scores * factor * step_j[q + h:q + h + 1, :]).astype(jnp.bfloat16))
                masked.append(jnp.where(lane_head == h, wide, 0.0).astype(jnp.bfloat16))
            within = jnp.dot(jnp.concatenate(weights, axis=1), jnp.concatenate(masked, axis=0),
                             preferred_element_type=jnp.float32)
            ybuf[r] = within + gain * wide
            ebuf[r] = by_head([turned[:, 16 + q + h:17 + q + h] for h in range(heads_dev)])
            tail = by_head([turned[:, 24 + q + h:25 + q + h] for h in range(heads_dev)])
            weighted = (wide * tail).astype(jnp.bfloat16)
            span_state[r] = lax.dot_general(b_part, weighted, (((0,), (0,)), ((), ())),
                                            preferred_element_type=jnp.float32)
            row_pass[r] = jnp.broadcast_to(by_head([pass_j[q + h:q + h + 1, :] for h in range(heads_dev)]),
                                           (8, width))

    do_peer(0)

    def arrive_odd_even(i, carry):
        j = 2 * i + 1
        x_copy(j).wait_recv()
        shared_arrival(j).wait_recv()
        do_peer(j)
        return carry

    def arrive_even(i, carry):
        x_copy(2 * i).wait_recv()
        do_peer(2 * i)
        return carry

    lax.fori_loop(1, half, arrive_even, 0)
    lax.fori_loop(0, half, arrive_odd_even, 0)

    def chain(k, carry):
        st, prod = carry
        r = source[k]
        incoming[k] = st
        prior_pass[k] = prod
        pass_r = row_pass[r]
        return pass_r[0:1] * st + span_state[r], prod * pass_r

    st, prod = lax.fori_loop(
        0, stream_rows, chain,
        (jnp.zeros((state, width), jnp.float32), jnp.ones((8, width), jnp.float32)))
    leave_out[0:state, :] = st
    leave_out[state:state + 8, :] = prod

    def start_leave(i, carry):
        leave_copy(i).start()
        return carry

    lax.fori_loop(1, ns, start_leave, 0)

    def wait_leave(i, carry):
        leave_copy(i).wait_recv()
        return carry

    lax.fori_loop(1, ns, wait_leave, 0)

    def enter(i, state_in):
        back = ns - 1 - i
        message = leave_in[back]
        following = message[state:state + 1, :] * state_in + message[0:state, :]
        return jnp.where(sq >= back, following, state_in)

    entering = lax.fori_loop(0, ns - 1, enter, jnp.zeros((state, width), jnp.float32))

    def finish(k, carry):
        r = source[k]
        carried = (incoming[k] + prior_pass[k][0:1] * entering).astype(jnp.bfloat16)
        c_part = shared_row(r)[:, state:]
        from_state = jnp.dot(c_part, carried, preferred_element_type=jnp.float32)
        out_ref[pl.ds(pl.multiple_of(k * row_len, row_len), row_len), :] = (
            ybuf[r] + from_state * ebuf[r]).astype(out_ref.dtype)
        return carry

    def shared_row(r):
        return sbuf[r // buffers, lax.rem(r, buffers)]

    lax.fori_loop(0, stream_rows, finish, 0)

    def end_buf(j, carry):
        x_copy(j).wait_send()
        step_copy(j).wait_send()
        meta_copy(j).wait_send()
        return carry

    def end_shared(i, carry):
        shared_copy(i).wait_send()
        forward_copy(i, sbuf.at[2 * i]).wait_send()
        return carry

    def end_leave(i, carry):
        leave_copy(i).wait_send()
        return carry

    lax.fori_loop(1, n, end_buf, 0)
    forward_copy(0, shared_ref).wait_send()
    lax.fori_loop(1, half, end_shared, 0)
    lax.fori_loop(1, ns, end_leave, 0)


def per_device(n, ns, row_inputs, row_shared, row_steps, row_count, row_slot, doc_start,
               decay_log, step_bias, skip_gain):
    buffers, row_len, inner = row_inputs.shape
    heads_dev = decay_log.shape[0]
    width = inner // n
    cols = row_shared.shape[2]
    state = cols // 2
    tokens = doc_start.shape[0]
    stream_rows = tokens // row_len
    total = n * buffers
    vmem = pl.BlockSpec(memory_space=pltpu.VMEM)
    smem = pl.BlockSpec(memory_space=pltpu.SMEM)
    hbm = pl.BlockSpec(memory_space=pl.ANY)
    f32, bf16, i32 = jnp.float32, jnp.bfloat16, jnp.int32
    dma = pltpu.SemaphoreType.DMA
    return pl.pallas_call(
        functools.partial(kernel, n, ns, heads_dev, stream_rows),
        out_shape=jax.ShapeDtypeStruct((tokens, width), bf16),
        in_specs=[hbm, hbm, vmem, smem, smem, vmem, smem, smem, smem],
        out_specs=vmem,
        scratch_shapes=[
            pltpu.VMEM((n, buffers, row_len, width), bf16),
            pltpu.VMEM((n, buffers, row_len, cols), bf16),
            pltpu.VMEM((n, 8, row_len), f32),
            pltpu.VMEM((n, 8, row_len), f32),
            pltpu.VMEM((8, 128), i32),
            pltpu.VMEM((n, 8, 128), i32),
            pltpu.SMEM((n, 8, 128), i32),
            pltpu.SMEM((stream_rows,), i32),
        ] + [pltpu.VMEM((n, 8, row_len), f32)] * 7 + [
            pltpu.VMEM((total, row_len, width), f32),
            pltpu.VMEM((total, row_len, width), f32),
            pltpu.VMEM((total, state, width), f32),
            pltpu.VMEM((total, 8, width), f32),
            pltpu.VMEM((stream_rows, state, width), f32),
            pltpu.VMEM((stream_rows, 8, width), f32),
            pltpu.VMEM((state + 8, width), f32),
            pltpu.VMEM((ns, state + 8, width), f32),
            dma((n,)), dma((n,)), dma((n,)), dma((n,)), dma((n,)),
            dma((n,)), dma((n,)), dma((n,)), dma((n,)), dma((ns,)), dma((ns,)), dma((3,)),
        ],
        compiler_params=pltpu.CompilerParams(
            collective_id=0, has_side_effects=True, vmem_limit_bytes=40 * 1024 * 1024),
    )(row_inputs, row_shared, row_steps, row_count, row_slot,
      doc_start.reshape(stream_rows, row_len), decay_log, step_bias, skip_gain)


def solution(mesh):
    return jax.shard_map(
        functools.partial(per_device, mesh.shape["buf"], mesh.shape["seq"]),
        mesh=mesh,
        in_specs=(
            P(("seq", "buf"), None, None),
            P(("seq", "buf"), None, None),
            P(("seq", "buf"), None, None),
            P(("seq", "buf")),
            P(("seq", "buf")),
            P("seq"),
            P("buf"),
            P("buf"),
            P("buf"),
        ),
        out_specs=P("seq", "buf"),
        check_vma=False,
    )
```

```python
import functools

import jax
import jax.numpy as jnp
from jax import lax
from jax.experimental import pallas as pl
from jax.experimental.pallas import tpu as pltpu
from jax.sharding import PartitionSpec as P

MESH = pl.DeviceIdType.MESH
EXACT = lax.Precision.HIGHEST


def softplus(value):
    small = jnp.exp(-jnp.abs(value))
    ratio = small / (small + 2.0)
    square = ratio * ratio
    series = jnp.full_like(ratio, 1.0 / 17.0)
    for odd in (15.0, 13.0, 11.0, 9.0, 7.0, 5.0, 3.0, 1.0):
        series = series * square + 1.0 / odd
    return jnp.maximum(value, 0.0) + 2.0 * ratio * series


def kernel(
    n, ns, heads_dev, stream_rows,
    inputs_ref, shared_ref, steps_ref, count_ref, slot_ref, doc_ref, log_ref, bias_ref, gain_ref,
    out_ref,
    xbuf, sbuf, step_out, step_in, meta_out, meta_in, meta_smem, source,
    docs, cums, counts_in, steps_q, enters, tails, passes,
    ybuf, ebuf, span_state, row_pass, incoming, prior_pass, leave_out, leave_in,
    x_send, x_recv, s_send, s_recv, f_send, st_send, st_recv, m_send, m_recv, l_send, l_recv, own_sem,
):
    me = lax.axis_index("buf")
    sq = lax.axis_index("seq")
    bit = lax.rem(me, 2)
    partner = me + 1 - 2 * bit
    buffers, row_len = steps_ref.shape[0], steps_ref.shape[2]
    width = xbuf.shape[3]
    head_size = width // heads_dev
    state = sbuf.shape[3] // 2
    half = n // 2

    barrier = pltpu.get_barrier_semaphore()

    def greet_buf(j, carry):
        pl.semaphore_signal(barrier, inc=1, device_id={"buf": lax.rem(me + j, n)}, device_id_type=MESH)
        return carry

    def greet_seq(j, carry):
        pl.semaphore_signal(barrier, inc=1, device_id={"seq": lax.rem(sq + j, ns)}, device_id_type=MESH)
        return carry

    lax.fori_loop(1, n, greet_buf, 0)
    lax.fori_loop(1, ns, greet_seq, 0)

    own_x = pltpu.make_async_copy(
        inputs_ref.at[:, :, pl.ds(pl.multiple_of(me * width, width), width)], xbuf.at[0], own_sem.at[0])
    own_s = pltpu.make_async_copy(shared_ref, sbuf.at[0], own_sem.at[1])
    own_x.start()
    own_s.start()

    step_out[...] = jnp.zeros_like(step_out)
    for b in range(buffers):
        turned = steps_ref[b].astype(jnp.float32)
        for g in range(n):
            step_out[g, b * heads_dev:(b + 1) * heads_dev, :] = turned[g * heads_dev:(g + 1) * heads_dev, :]
    count = count_ref[0]
    row_id = lax.broadcasted_iota(jnp.int32, meta_out.shape, 1)
    meta = jnp.full(meta_out.shape, stream_rows, jnp.int32)
    for b in range(buffers):
        slot = jnp.clip(slot_ref[b] - sq * stream_rows, 0, stream_rows - 1)
        meta = jnp.where(row_id == b, jnp.where(b < count, slot, stream_rows), meta)
    meta_out[...] = meta
    meta_in[0] = meta
    step_in[0] = step_out[me]

    pl.semaphore_wait(barrier, n - 1 + ns - 1)

    def x_copy(j):
        peer = lax.rem(me + j, n)
        return pltpu.make_async_remote_copy(
            src_ref=inputs_ref.at[:, :, pl.ds(pl.multiple_of(peer * width, width), width)],
            dst_ref=xbuf.at[j], send_sem=x_send.at[j], recv_sem=x_recv.at[j],
            device_id={"buf": peer}, device_id_type=MESH)

    def step_copy(j):
        peer = lax.rem(me + j, n)
        return pltpu.make_async_remote_copy(
            src_ref=step_out.at[peer], dst_ref=step_in.at[j], send_sem=st_send.at[j], recv_sem=st_recv.at[j],
            device_id={"buf": peer}, device_id_type=MESH)

    def meta_copy(j):
        peer = lax.rem(me + j, n)
        return pltpu.make_async_remote_copy(
            src_ref=meta_out, dst_ref=meta_in.at[j], send_sem=m_send.at[j], recv_sem=m_recv.at[j],
            device_id={"buf": peer}, device_id_type=MESH)

    def shared_copy(i):
        peer = lax.rem(me + 2 * i, n)
        return pltpu.make_async_remote_copy(
            src_ref=shared_ref, dst_ref=sbuf.at[2 * i], send_sem=s_send.at[i], recv_sem=s_recv.at[2 * i],
            device_id={"buf": peer}, device_id_type=MESH)

    def forward_copy(i, src):
        slot = lax.rem(2 * i + 1 - 2 * bit + n, n)
        return pltpu.make_async_remote_copy(
            src_ref=src, dst_ref=sbuf.at[slot], send_sem=f_send.at[i], recv_sem=s_recv.at[slot],
            device_id={"buf": partner}, device_id_type=MESH)

    def shared_arrival(j):
        return pltpu.make_async_remote_copy(
            src_ref=shared_ref, dst_ref=sbuf.at[j], send_sem=f_send.at[0], recv_sem=s_recv.at[j],
            device_id={"buf": partner}, device_id_type=MESH)

    def leave_copy(i):
        return pltpu.make_async_remote_copy(
            src_ref=leave_out, dst_ref=leave_in.at[i], send_sem=l_send.at[i], recv_sem=l_recv.at[i],
            device_id={"seq": lax.rem(sq + i, ns)}, device_id_type=MESH)

    def start_small(j, carry):
        meta_copy(j).start()
        step_copy(j).start()
        return carry

    def start_shared(i, carry):
        shared_copy(i).start()
        return carry

    def start_x(j, carry):
        x_copy(j).start()
        return carry

    lax.fori_loop(1, n, start_small, 0)
    lax.fori_loop(1, half, start_shared, 0)
    forward_copy(0, shared_ref).start()
    lax.fori_loop(1, half, lambda i, c: start_x(2 * i, c), 0)
    lax.fori_loop(0, half, lambda i, c: start_x(2 * i + 1, c), 0)

    def wait_small(j, carry):
        meta_copy(j).wait_recv()
        step_copy(j).wait_recv()
        return carry

    lax.fori_loop(1, n, wait_small, 0)
    to_scalar = pltpu.make_async_copy(meta_in, meta_smem, own_sem.at[2])
    to_scalar.start()

    def pass_on(i, carry):
        shared_arrival(2 * i).wait_recv()
        forward_copy(i, sbuf.at[2 * i]).start()
        return carry

    lax.fori_loop(1, half, pass_on, 0)

    shape = (n * 8, row_len)
    tri_up = (lax.broadcasted_iota(jnp.int32, (row_len, row_len), 0)
              <= lax.broadcasted_iota(jnp.int32, (row_len, row_len), 1)).astype(jnp.float32)
    head_row = lax.rem(lax.broadcasted_iota(jnp.int32, shape, 0), heads_dev)
    bias = jnp.full(shape, bias_ref[0], jnp.float32)
    decay = jnp.full(shape, log_ref[0], jnp.float32)
    for h in range(1, heads_dev):
        bias = jnp.where(head_row == h, bias_ref[h], bias)
        decay = jnp.where(head_row == h, log_ref[h], decay)
    step = softplus(step_in[...].reshape(shape) + bias)
    cum = jnp.dot(-step * jnp.exp(decay), tri_up, precision=EXACT, preferred_element_type=jnp.float32)

    to_scalar.wait()
    docs[...] = jnp.zeros_like(docs)

    def put_docs(j, carry):
        for b in range(buffers):
            slot = jnp.minimum(meta_smem[j, 0, b], stream_rows - 1)
            line = doc_ref[pl.ds(slot, 1), :].astype(jnp.float32)
            docs[j, b * heads_dev:(b + 1) * heads_dev, :] = jnp.broadcast_to(line, (heads_dev, row_len))
        return carry

    lax.fori_loop(0, n, put_docs, 0)

    def put_source(k, carry):
        found = jnp.int32(0)
        for j in range(n):
            for b in range(buffers):
                found = found + jnp.where(meta_smem[j, 0, b] == k, j * buffers + b, 0)
        source[k] = found
        return carry

    lax.fori_loop(0, stream_rows, put_source, 0)

    resets = jnp.dot(docs[...].reshape(shape), tri_up, precision=EXACT, preferred_element_type=jnp.float32)
    last_cum = cum[:, row_len - 1:row_len]
    last_resets = resets[:, row_len - 1:row_len]
    cube = (n, 8, row_len)
    cums[...] = cum.reshape(cube)
    counts_in[...] = resets.reshape(cube)
    steps_q[...] = step.reshape(cube)
    enters[...] = jnp.where(resets == 0.0, jnp.exp(cum), 0.0).reshape(cube)
    tails[...] = (jnp.where(resets == last_resets, jnp.exp(last_cum - cum), 0.0) * step).reshape(cube)
    passes[...] = jnp.broadcast_to(
        jnp.where(last_resets == 0.0, jnp.exp(last_cum), 0.0), shape).reshape(cube)

    own_s.wait()
    own_x.wait()

    lower = (lax.broadcasted_iota(jnp.int32, (row_len, row_len), 0)
             >= lax.broadcasted_iota(jnp.int32, (row_len, row_len), 1))
    lane_head = lax.broadcasted_iota(jnp.int32, (1, width), 1) // head_size
    gain = jnp.full((1, width), gain_ref[0], jnp.float32)
    for h in range(1, heads_dev):
        gain = jnp.where(lane_head == h, gain_ref[h], gain)

    def by_head(parts):
        full = jnp.broadcast_to(parts[0], (parts[0].shape[0], width))
        for h in range(1, heads_dev):
            full = jnp.where(lane_head == h, parts[h], full)
        return full

    def do_peer(j):
        cum_j = cums[j]
        resets_j = counts_in[j]
        step_j = steps_q[j]
        pass_j = passes[j]
        turned = jnp.concatenate([cum_j, resets_j, enters[j], tails[j]], axis=0).T
        for b in range(buffers):
            r = j * buffers + b
            x = xbuf[j, b]
            wide = x.astype(jnp.float32)
            b_part = sbuf[j, b, :, :state]
            c_part = sbuf[j, b, :, state:]
            scores = lax.dot_general(c_part, b_part, (((1,), (1,)), ((), ())),
                                     preferred_element_type=jnp.float32)
            q = b * heads_dev
            together = lower & (turned[:, 8 + q:9 + q] == resets_j[q:q + 1, :])
            weights = []
            masked = []
            for h in range(heads_dev):
                gap = turned[:, q + h:q + h + 1] - cum_j[q + h:q + h + 1, :]
                factor = jnp.exp(jnp.where(together, gap, -1e30))
                weights.append((scores * factor * step_j[q + h:q + h + 1, :]).astype(jnp.bfloat16))
                masked.append(jnp.where(lane_head == h, wide, 0.0).astype(jnp.bfloat16))
            within = jnp.dot(jnp.concatenate(weights, axis=1), jnp.concatenate(masked, axis=0),
                             preferred_element_type=jnp.float32)
            ybuf[r] = within + gain * wide
            ebuf[r] = by_head([turned[:, 16 + q + h:17 + q + h] for h in range(heads_dev)])
            tail = by_head([turned[:, 24 + q + h:25 + q + h] for h in range(heads_dev)])
            weighted = (wide * tail).astype(jnp.bfloat16)
            span_state[r] = lax.dot_general(b_part, weighted, (((0,), (0,)), ((), ())),
                                            preferred_element_type=jnp.float32)
            row_pass[r] = jnp.broadcast_to(by_head([pass_j[q + h:q + h + 1, :] for h in range(heads_dev)]),
                                           (8, width))

    do_peer(0)

    def arrive_odd_even(i, carry):
        j = 2 * i + 1
        x_copy(j).wait_recv()
        shared_arrival(j).wait_recv()
        do_peer(j)
        return carry

    def arrive_even(i, carry):
        x_copy(2 * i).wait_recv()
        do_peer(2 * i)
        return carry

    lax.fori_loop(1, half, arrive_even, 0)
    lax.fori_loop(0, half, arrive_odd_even, 0)

    def chain(k, carry):
        st, prod = carry
        r = source[k]
        incoming[k] = st
        prior_pass[k] = prod
        pass_r = row_pass[r]
        return pass_r[0:1] * st + span_state[r], prod * pass_r

    def chain_some(i, carry):
        for u in range(6):
            carry = chain(6 * i + u, carry)
        return carry

    st, prod = lax.fori_loop(
        0, stream_rows // 6, chain_some,
        (jnp.zeros((state, width), jnp.float32), jnp.ones((8, width), jnp.float32)))
    leave_out[0:state, :] = st
    leave_out[state:state + 8, :] = prod

    def start_leave(i, carry):
        leave_copy(i).start()
        return carry

    lax.fori_loop(1, ns - sq, start_leave, 0)

    def wait_leave(i, carry):
        leave_copy(i).wait_recv()
        return carry

    lax.fori_loop(1, sq + 1, wait_leave, 0)

    def enter(i, state_in):
        back = sq - i
        message = leave_in[back]
        following = message[state:state + 1, :] * state_in + message[0:state, :]
        return following

    entering = lax.fori_loop(0, sq, enter, jnp.zeros((state, width), jnp.float32))

    def finish(k, carry):
        r = source[k]
        carried = (incoming[k] + prior_pass[k][0:1] * entering).astype(jnp.bfloat16)
        c_part = shared_row(r)[:, state:]
        from_state = jnp.dot(c_part, carried, preferred_element_type=jnp.float32)
        out_ref[pl.ds(pl.multiple_of(k * row_len, row_len), row_len), :] = (
            ybuf[r] + from_state * ebuf[r]).astype(out_ref.dtype)
        return carry

    def shared_row(r):
        return sbuf[r // buffers, lax.rem(r, buffers)]

    def finish_some(i, carry):
        for u in range(6):
            finish(6 * i + u, 0)
        return carry

    lax.fori_loop(0, stream_rows // 6, finish_some, 0)

    def end_buf(j, carry):
        x_copy(j).wait_send()
        step_copy(j).wait_send()
        meta_copy(j).wait_send()
        return carry

    def end_shared(i, carry):
        shared_copy(i).wait_send()
        forward_copy(i, sbuf.at[2 * i]).wait_send()
        return carry

    def end_leave(i, carry):
        leave_copy(i).wait_send()
        return carry

    lax.fori_loop(1, n, end_buf, 0)
    forward_copy(0, shared_ref).wait_send()
    lax.fori_loop(1, half, end_shared, 0)
    lax.fori_loop(1, ns - sq, end_leave, 0)


def per_device(n, ns, row_inputs, row_shared, row_steps, row_count, row_slot, doc_start,
               decay_log, step_bias, skip_gain):
    buffers, row_len, inner = row_inputs.shape
    heads_dev = decay_log.shape[0]
    width = inner // n
    cols = row_shared.shape[2]
    state = cols // 2
    tokens = doc_start.shape[0]
    stream_rows = tokens // row_len
    total = n * buffers
    vmem = pl.BlockSpec(memory_space=pltpu.VMEM)
    smem = pl.BlockSpec(memory_space=pltpu.SMEM)
    hbm = pl.BlockSpec(memory_space=pl.ANY)
    f32, bf16, i32 = jnp.float32, jnp.bfloat16, jnp.int32
    dma = pltpu.SemaphoreType.DMA
    return pl.pallas_call(
        functools.partial(kernel, n, ns, heads_dev, stream_rows),
        out_shape=jax.ShapeDtypeStruct((tokens, width), bf16),
        in_specs=[hbm, hbm, vmem, smem, smem, vmem, smem, smem, smem],
        out_specs=vmem,
        scratch_shapes=[
            pltpu.VMEM((n, buffers, row_len, width), bf16),
            pltpu.VMEM((n, buffers, row_len, cols), bf16),
            pltpu.VMEM((n, 8, row_len), f32),
            pltpu.VMEM((n, 8, row_len), f32),
            pltpu.VMEM((1, 128), i32),
            pltpu.VMEM((n, 1, 128), i32),
            pltpu.SMEM((n, 1, 128), i32),
            pltpu.SMEM((stream_rows,), i32),
        ] + [pltpu.VMEM((n, 8, row_len), f32)] * 7 + [
            pltpu.VMEM((total, row_len, width), f32),
            pltpu.VMEM((total, row_len, width), f32),
            pltpu.VMEM((total, state, width), f32),
            pltpu.VMEM((total, 8, width), f32),
            pltpu.VMEM((stream_rows, state, width), f32),
            pltpu.VMEM((stream_rows, 8, width), f32),
            pltpu.VMEM((state + 8, width), f32),
            pltpu.VMEM((ns, state + 8, width), f32),
            dma((n,)), dma((n,)), dma((n,)), dma((n,)), dma((n,)),
            dma((n,)), dma((n,)), dma((n,)), dma((n,)), dma((ns,)), dma((ns,)), dma((3,)),
        ],
        compiler_params=pltpu.CompilerParams(
            collective_id=0, has_side_effects=True, vmem_limit_bytes=60 * 1024 * 1024),
    )(row_inputs, row_shared, row_steps.transpose(0, 2, 1), row_count, row_slot,
      doc_start.reshape(stream_rows, row_len), decay_log, step_bias, skip_gain)


def solution(mesh):
    return jax.shard_map(
        functools.partial(per_device, mesh.shape["buf"], mesh.shape["seq"]),
        mesh=mesh,
        in_specs=(
            P(("seq", "buf"), None, None),
            P(("seq", "buf"), None, None),
            P(("seq", "buf"), None, None),
            P(("seq", "buf")),
            P(("seq", "buf")),
            P("seq"),
            P("buf"),
            P("buf"),
            P("buf"),
        ),
        out_specs=P("seq", "buf"),
        check_vma=False,
    )
```

```python
import functools

import jax
import jax.numpy as jnp
from jax import lax
from jax.experimental import pallas as pl
from jax.experimental.pallas import tpu as pltpu
from jax.sharding import PartitionSpec as P

MESH = pl.DeviceIdType.MESH
EXACT = lax.Precision.HIGHEST


def softplus(value):
    small = jnp.exp(-jnp.abs(value))
    ratio = small / (small + 2.0)
    square = ratio * ratio
    series = jnp.full_like(ratio, 1.0 / 17.0)
    for odd in (15.0, 13.0, 11.0, 9.0, 7.0, 5.0, 3.0, 1.0):
        series = series * square + 1.0 / odd
    return jnp.maximum(value, 0.0) + 2.0 * ratio * series


def kernel(
    n, ns, heads_dev, stream_rows,
    inputs_ref, shared_ref, steps_ref, count_ref, slot_ref, doc_ref, log_ref, bias_ref, gain_ref,
    result_ref,
    out_ref, out_sem, xbuf, sbuf, step_out, step_in, meta_out, meta_in, meta_smem, source,
    docs, cums, counts_in, steps_q, enters, tails, passes,
    ybuf, ebuf, span_state, row_pass, incoming, prior_pass, leave_out, leave_in,
    x_send, x_recv, s_send, s_recv, f_send, st_send, st_recv, m_send, m_recv, l_send, l_recv, own_sem,
):
    me = lax.axis_index("buf")
    sq = lax.axis_index("seq")
    bit = lax.rem(me, 2)
    partner = me + 1 - 2 * bit
    buffers, row_len = steps_ref.shape[0], steps_ref.shape[2]
    width = xbuf.shape[3]
    head_size = width // heads_dev
    state = sbuf.shape[3] // 2
    half = n // 2

    barrier = pltpu.get_barrier_semaphore()

    def greet_buf(j, carry):
        pl.semaphore_signal(barrier, inc=1, device_id={"buf": lax.rem(me + j, n)}, device_id_type=MESH)
        return carry

    def greet_seq(j, carry):
        pl.semaphore_signal(barrier, inc=1, device_id={"seq": lax.rem(sq + j, ns)}, device_id_type=MESH)
        return carry

    lax.fori_loop(1, n, greet_buf, 0)
    lax.fori_loop(1, ns, greet_seq, 0)

    own_x = pltpu.make_async_copy(
        inputs_ref.at[:, :, pl.ds(pl.multiple_of(me * width, width), width)], xbuf.at[0], own_sem.at[0])
    own_s = pltpu.make_async_copy(shared_ref, sbuf.at[0], own_sem.at[1])
    own_x.start()
    own_s.start()

    step_out[...] = jnp.zeros_like(step_out)
    for b in range(buffers):
        turned = steps_ref[b].astype(jnp.float32)
        for g in range(n):
            step_out[g, b * heads_dev:(b + 1) * heads_dev, :] = turned[g * heads_dev:(g + 1) * heads_dev, :]
    count = count_ref[0]
    row_id = lax.broadcasted_iota(jnp.int32, meta_out.shape, 1)
    meta = jnp.full(meta_out.shape, stream_rows, jnp.int32)
    for b in range(buffers):
        slot = jnp.clip(slot_ref[b] - sq * stream_rows, 0, stream_rows - 1)
        meta = jnp.where(row_id == b, jnp.where(b < count, slot, stream_rows), meta)
    meta_out[...] = meta
    meta_in[0] = meta
    step_in[0] = step_out[me]

    pl.semaphore_wait(barrier, n - 1 + ns - 1)

    def x_copy(j):
        peer = lax.rem(me + j, n)
        return pltpu.make_async_remote_copy(
            src_ref=inputs_ref.at[:, :, pl.ds(pl.multiple_of(peer * width, width), width)],
            dst_ref=xbuf.at[j], send_sem=x_send.at[j], recv_sem=x_recv.at[j],
            device_id={"buf": peer}, device_id_type=MESH)

    def step_copy(j):
        peer = lax.rem(me + j, n)
        return pltpu.make_async_remote_copy(
            src_ref=step_out.at[peer], dst_ref=step_in.at[j], send_sem=st_send.at[j], recv_sem=st_recv.at[j],
            device_id={"buf": peer}, device_id_type=MESH)

    def meta_copy(j):
        peer = lax.rem(me + j, n)
        return pltpu.make_async_remote_copy(
            src_ref=meta_out, dst_ref=meta_in.at[j], send_sem=m_send.at[j], recv_sem=m_recv.at[j],
            device_id={"buf": peer}, device_id_type=MESH)

    def shared_copy(i):
        peer = lax.rem(me + 2 * i, n)
        return pltpu.make_async_remote_copy(
            src_ref=shared_ref, dst_ref=sbuf.at[2 * i], send_sem=s_send.at[i], recv_sem=s_recv.at[2 * i],
            device_id={"buf": peer}, device_id_type=MESH)

    def forward_copy(i, src):
        slot = lax.rem(2 * i + 1 - 2 * bit + n, n)
        return pltpu.make_async_remote_copy(
            src_ref=src, dst_ref=sbuf.at[slot], send_sem=f_send.at[i], recv_sem=s_recv.at[slot],
            device_id={"buf": partner}, device_id_type=MESH)

    def shared_arrival(j):
        return pltpu.make_async_remote_copy(
            src_ref=shared_ref, dst_ref=sbuf.at[j], send_sem=f_send.at[0], recv_sem=s_recv.at[j],
            device_id={"buf": partner}, device_id_type=MESH)

    def leave_copy(i):
        return pltpu.make_async_remote_copy(
            src_ref=leave_out, dst_ref=leave_in.at[i], send_sem=l_send.at[i], recv_sem=l_recv.at[i],
            device_id={"seq": lax.rem(sq + i, ns)}, device_id_type=MESH)

    def start_small(j, carry):
        meta_copy(j).start()
        step_copy(j).start()
        return carry

    def start_shared(i, carry):
        shared_copy(i).start()
        return carry

    def start_x(j, carry):
        x_copy(j).start()
        return carry

    lax.fori_loop(1, n, start_small, 0)
    lax.fori_loop(1, half, start_shared, 0)
    forward_copy(0, shared_ref).start()
    lax.fori_loop(1, n, start_x, 0)

    def wait_small(j, carry):
        meta_copy(j).wait_recv()
        step_copy(j).wait_recv()
        return carry

    lax.fori_loop(1, n, wait_small, 0)
    to_scalar = pltpu.make_async_copy(meta_in, meta_smem, own_sem.at[2])
    to_scalar.start()

    def pass_on(i, carry):
        shared_arrival(2 * i).wait_recv()
        forward_copy(i, sbuf.at[2 * i]).start()
        return carry

    lax.fori_loop(1, half, pass_on, 0)

    shape = (n * 8, row_len)
    tri_up = (lax.broadcasted_iota(jnp.int32, (row_len, row_len), 0)
              <= lax.broadcasted_iota(jnp.int32, (row_len, row_len), 1)).astype(jnp.float32)
    head_row = lax.rem(lax.broadcasted_iota(jnp.int32, shape, 0), heads_dev)
    bias = jnp.full(shape, bias_ref[0], jnp.float32)
    decay = jnp.full(shape, log_ref[0], jnp.float32)
    for h in range(1, heads_dev):
        bias = jnp.where(head_row == h, bias_ref[h], bias)
        decay = jnp.where(head_row == h, log_ref[h], decay)
    step = softplus(step_in[...].reshape(shape) + bias)
    cum = jnp.dot(-step * jnp.exp(decay), tri_up, precision=EXACT, preferred_element_type=jnp.float32)

    to_scalar.wait()
    docs[...] = jnp.zeros_like(docs)

    def put_docs(j, carry):
        for b in range(buffers):
            slot = jnp.minimum(meta_smem[j, 0, b], stream_rows - 1)
            line = doc_ref[pl.ds(slot, 1), :].astype(jnp.float32)
            docs[j, b * heads_dev:(b + 1) * heads_dev, :] = jnp.broadcast_to(line, (heads_dev, row_len))
        return carry

    lax.fori_loop(0, n, put_docs, 0)

    def put_source(k, carry):
        found = jnp.int32(0)
        for j in range(n):
            for b in range(buffers):
                found = found + jnp.where(meta_smem[j, 0, b] == k, j * buffers + b, 0)
        source[k] = found
        return carry

    lax.fori_loop(0, stream_rows, put_source, 0)

    resets = jnp.dot(docs[...].reshape(shape), tri_up, precision=EXACT, preferred_element_type=jnp.float32)
    last_cum = cum[:, row_len - 1:row_len]
    last_resets = resets[:, row_len - 1:row_len]
    cube = (n, 8, row_len)
    cums[...] = cum.reshape(cube)
    counts_in[...] = resets.reshape(cube)
    steps_q[...] = step.reshape(cube)
    enters[...] = jnp.where(resets == 0.0, jnp.exp(cum), 0.0).reshape(cube)
    tails[...] = (jnp.where(resets == last_resets, jnp.exp(last_cum - cum), 0.0) * step).reshape(cube)
    passes[...] = jnp.broadcast_to(
        jnp.where(last_resets == 0.0, jnp.exp(last_cum), 0.0), shape).reshape(cube)

    own_s.wait()
    own_x.wait()

    lower = (lax.broadcasted_iota(jnp.int32, (row_len, row_len), 0)
             >= lax.broadcasted_iota(jnp.int32, (row_len, row_len), 1))
    lane_head = lax.broadcasted_iota(jnp.int32, (1, width), 1) // head_size
    gain = jnp.full((1, width), gain_ref[0], jnp.float32)
    for h in range(1, heads_dev):
        gain = jnp.where(lane_head == h, gain_ref[h], gain)

    def by_head(parts):
        full = jnp.broadcast_to(parts[0], (parts[0].shape[0], width))
        for h in range(1, heads_dev):
            full = jnp.where(lane_head == h, parts[h], full)
        return full

    def do_peer(j):
        cum_j = cums[j]
        resets_j = counts_in[j]
        step_j = steps_q[j]
        pass_j = passes[j]
        turned = jnp.concatenate([cum_j, resets_j, enters[j], tails[j]], axis=0).T
        for b in range(buffers):
            r = j * buffers + b
            x = xbuf[j, b]
            wide = x.astype(jnp.float32)
            b_part = sbuf[j, b, :, :state]
            c_part = sbuf[j, b, :, state:]
            scores = lax.dot_general(c_part, b_part, (((1,), (1,)), ((), ())),
                                     preferred_element_type=jnp.float32)
            q = b * heads_dev
            together = lower & (turned[:, 8 + q:9 + q] == resets_j[q:q + 1, :])
            weights = []
            masked = []
            for h in range(heads_dev):
                gap = turned[:, q + h:q + h + 1] - cum_j[q + h:q + h + 1, :]
                factor = jnp.exp(jnp.where(together, gap, -1e30))
                weights.append((scores * factor * step_j[q + h:q + h + 1, :]).astype(jnp.bfloat16))
                masked.append(jnp.where(lane_head == h, wide, 0.0).astype(jnp.bfloat16))
            within = jnp.dot(jnp.concatenate(weights, axis=1), jnp.concatenate(masked, axis=0),
                             preferred_element_type=jnp.float32)
            ybuf[r] = within + gain * wide
            ebuf[r] = by_head([turned[:, 16 + q + h:17 + q + h] for h in range(heads_dev)])
            tail = by_head([turned[:, 24 + q + h:25 + q + h] for h in range(heads_dev)])
            weighted = (wide * tail).astype(jnp.bfloat16)
            span_state[r] = lax.dot_general(b_part, weighted, (((0,), (0,)), ((), ())),
                                            preferred_element_type=jnp.float32)
            row_pass[r] = jnp.broadcast_to(by_head([pass_j[q + h:q + h + 1, :] for h in range(heads_dev)]),
                                           (8, width))

    do_peer(0)

    def arrive_odd_even(i, carry):
        j = 2 * i + 1
        x_copy(j).wait_recv()
        shared_arrival(j).wait_recv()
        do_peer(j)
        return carry

    def arrive_even(i, carry):
        x_copy(2 * i).wait_recv()
        do_peer(2 * i)
        return carry

    lax.fori_loop(1, half, arrive_even, 0)
    lax.fori_loop(0, half, arrive_odd_even, 0)

    def chain(k, carry):
        st, prod = carry
        r = source[k]
        incoming[k] = st
        prior_pass[k] = prod
        pass_r = row_pass[r]
        return pass_r[0:1] * st + span_state[r], prod * pass_r

    def chain_some(i, carry):
        for u in range(6):
            carry = chain(6 * i + u, carry)
        return carry

    st, prod = lax.fori_loop(
        0, stream_rows // 6, chain_some,
        (jnp.zeros((state, width), jnp.float32), jnp.ones((8, width), jnp.float32)))
    leave_out[0:state, :] = st
    leave_out[state:state + 8, :] = prod

    def start_leave(i, carry):
        leave_copy(i).start()
        return carry

    lax.fori_loop(1, ns - sq, start_leave, 0)

    def wait_leave(i, carry):
        leave_copy(i).wait_recv()
        return carry

    lax.fori_loop(1, sq + 1, wait_leave, 0)

    def enter(i, state_in):
        back = sq - i
        message = leave_in[back]
        following = message[state:state + 1, :] * state_in + message[0:state, :]
        return following

    entering = lax.fori_loop(0, sq, enter, jnp.zeros((state, width), jnp.float32))

    def finish(k, carry):
        r = source[k]
        carried = (incoming[k] + prior_pass[k][0:1] * entering).astype(jnp.bfloat16)
        c_part = shared_row(r)[:, state:]
        from_state = jnp.dot(c_part, carried, preferred_element_type=jnp.float32)
        out_ref[pl.ds(pl.multiple_of(k * row_len, row_len), row_len), :] = (
            ybuf[r] + from_state * ebuf[r]).astype(out_ref.dtype)
        return carry

    def shared_row(r):
        return sbuf[r // buffers, lax.rem(r, buffers)]

    def out_copy(i):
        part = pl.ds(pl.multiple_of(i * 6 * row_len, row_len), 6 * row_len)
        return pltpu.make_async_copy(out_ref.at[part, :], result_ref.at[part, :], out_sem.at[i])

    def end_out(i, carry):
        out_copy(i).wait()
        return carry

    def finish_some(i, carry):
        for u in range(6):
            finish(6 * i + u, 0)
        out_copy(i).start()
        return carry

    lax.fori_loop(0, stream_rows // 6, finish_some, 0)

    def end_buf(j, carry):
        x_copy(j).wait_send()
        step_copy(j).wait_send()
        meta_copy(j).wait_send()
        return carry

    def end_shared(i, carry):
        shared_copy(i).wait_send()
        forward_copy(i, sbuf.at[2 * i]).wait_send()
        return carry

    def end_leave(i, carry):
        leave_copy(i).wait_send()
        return carry

    lax.fori_loop(1, n, end_buf, 0)
    lax.fori_loop(0, stream_rows // 6, end_out, 0)
    forward_copy(0, shared_ref).wait_send()
    lax.fori_loop(1, half, end_shared, 0)
    lax.fori_loop(1, ns - sq, end_leave, 0)


def per_device(n, ns, row_inputs, row_shared, row_steps, row_count, row_slot, doc_start,
               decay_log, step_bias, skip_gain):
    buffers, row_len, inner = row_inputs.shape
    heads_dev = decay_log.shape[0]
    width = inner // n
    cols = row_shared.shape[2]
    state = cols // 2
    tokens = doc_start.shape[0]
    stream_rows = tokens // row_len
    total = n * buffers
    vmem = pl.BlockSpec(memory_space=pltpu.VMEM)
    smem = pl.BlockSpec(memory_space=pltpu.SMEM)
    hbm = pl.BlockSpec(memory_space=pl.ANY)
    f32, bf16, i32 = jnp.float32, jnp.bfloat16, jnp.int32
    dma = pltpu.SemaphoreType.DMA
    return pl.pallas_call(
        functools.partial(kernel, n, ns, heads_dev, stream_rows),
        out_shape=jax.ShapeDtypeStruct((tokens, width), bf16),
        in_specs=[hbm, hbm, vmem, smem, smem, vmem, smem, smem, smem],
        out_specs=hbm,
        scratch_shapes=[
            pltpu.VMEM((tokens, width), bf16),
            dma((stream_rows // 6,)),
            pltpu.VMEM((n, buffers, row_len, width), bf16),
            pltpu.VMEM((n, buffers, row_len, cols), bf16),
            pltpu.VMEM((n, 8, row_len), f32),
            pltpu.VMEM((n, 8, row_len), f32),
            pltpu.VMEM((1, 128), i32),
            pltpu.VMEM((n, 1, 128), i32),
            pltpu.SMEM((n, 1, 128), i32),
            pltpu.SMEM((stream_rows,), i32),
        ] + [pltpu.VMEM((n, 8, row_len), f32)] * 7 + [
            pltpu.VMEM((total, row_len, width), f32),
            pltpu.VMEM((total, row_len, width), f32),
            pltpu.VMEM((total, state, width), f32),
            pltpu.VMEM((total, 8, width), f32),
            pltpu.VMEM((stream_rows, state, width), f32),
            pltpu.VMEM((stream_rows, 8, width), f32),
            pltpu.VMEM((state + 8, width), f32),
            pltpu.VMEM((ns, state + 8, width), f32),
            dma((n,)), dma((n,)), dma((n,)), dma((n,)), dma((n,)),
            dma((n,)), dma((n,)), dma((n,)), dma((n,)), dma((ns,)), dma((ns,)), dma((3,)),
        ],
        compiler_params=pltpu.CompilerParams(
            collective_id=0, has_side_effects=True, vmem_limit_bytes=60 * 1024 * 1024),
    )(row_inputs, row_shared, row_steps.transpose(0, 2, 1), row_count, row_slot,
      doc_start.reshape(stream_rows, row_len), decay_log, step_bias, skip_gain)


def solution(mesh):
    return jax.shard_map(
        functools.partial(per_device, mesh.shape["buf"], mesh.shape["seq"]),
        mesh=mesh,
        in_specs=(
            P(("seq", "buf"), None, None),
            P(("seq", "buf"), None, None),
            P(("seq", "buf"), None, None),
            P(("seq", "buf")),
            P(("seq", "buf")),
            P("seq"),
            P("buf"),
            P("buf"),
            P("buf"),
        ),
        out_specs=P("seq", "buf"),
        check_vma=False,
    )
```
